32 devices in a mesh: ctx: 8 (over z, y), tp: 4 (over x, core).
Axes of the slice: x: 2, y: 2, z: 4, core: 2. Of those that a mesh axis runs over, the one named last changes fastest.
Arguments:
- features: bfloat16 [3, 2048, 1024], P(None, 'tp', 'ctx'), may hold values from -6 to 6
- short_taps: float32 [3, 3, 2048], P(None, None, 'tp'), may hold values from -3 to 3
- filters: bfloat16 [128, 1024], P('tp'), may hold values from -2 to 2
- skip_gain: float32 [2048], P('tp'), may hold values from -4 to 4
- out_weight: bfloat16 [2048, 2048], P('tp'), may hold values from -0.125 to 0.125
Outputs:
- block_out: bfloat16 [2048, 1024], P('tp', 'ctx')
The draws below stay inside these ranges and needn't reach their ends.
All inputs are finite; a program needn't handle non-finite values.
Results may differ from the reference program's by a relative error of at most 0.009.
Values may be sent and summed in bfloat16 or wider, within the bound.
A program may use at most 64 MiB of HBM per device.

```python
import math
import jax
import jax.numpy as jnp
from jax import lax

CH = 2048
OUT = 2048
GROUP = 16
TAPS = 3
GROUPS = 128
TOKENS = 1024
N_TP = 4


def draw_filters(key, part):
    rate_key, value_key = jax.random.split(jax.random.fold_in(key, 17))
    position = jnp.arange(TOKENS, dtype=jnp.float32)
    log_span = jax.random.uniform(rate_key, (GROUPS, 1), minval=math.log(30.0), maxval=math.log(TOKENS * 4.0))
    values = jax.random.normal(value_key, (GROUPS, TOKENS))
    span_len = jnp.exp(log_span)
    envelope = jnp.exp(-position[None, :] / span_len)
    energy = (1.0 - jnp.exp(-2.0 / span_len)) / (1.0 - jnp.exp(-2.0 * TOKENS / span_len))
    return (values * envelope * jnp.sqrt(energy)).astype(jnp.float32).astype(jnp.bfloat16)


def steps_of(own_key, dims, pieces, least, largest):
    loudness = 1.0
    for dim, shards_of in pieces:
        steps = jax.random.uniform(jax.random.fold_in(jax.random.fold_in(own_key, 6), dim), (shards_of,), jnp.float32, least / len(pieces), largest / len(pieces))
        loudness = loudness * jnp.repeat(jnp.exp(steps), dims[dim] // shards_of).reshape((-1,) + (1,) * (len(dims) - 1 - dim))
    return loudness


def scatter_about(stream_key, dims, deviation, bound, shards=(), kind=jnp.bfloat16):
    array = deviation * jax.random.normal(stream_key, dims, jnp.float32)
    if shards:
        array = array * steps_of(stream_key, dims, shards, -0.22, 0.18)
    return jnp.clip(array, -bound, bound).astype(kind)


def setup_inputs(seed: int = 0) -> dict:
    streams_of = jax.random.split(jax.random.key(seed), 6)
    return {
        "features": scatter_about(streams_of[0], (3, CH, TOKENS), 1.0, 6.0, ((1, 4), (2, 8))),
        "short_taps": scatter_about(streams_of[1], (TAPS, 3, CH), 0.6, 3.0, ((2, 4),), jnp.float32),
        "filters": draw_filters(jax.random.fold_in(streams_of[5], 71), 0),
        "skip_gain": scatter_about(streams_of[3], (CH,), 1.0, 4.0, ((0, 4),), jnp.float32),
        "out_weight": scatter_about(streams_of[4], (CH, OUT), CH ** -0.5, 0.125, ((0, 4),)),
    }


def short_conv(features, short_taps):
    taps_count = short_taps.shape[0]
    values = features.astype(jnp.float32)
    padded = jnp.pad(values, ((0, 0), (0, 0), (taps_count - 1, 0)))
    length = values.shape[2]
    result = jnp.zeros(values.shape, jnp.float32)
    for offset in range(taps_count):
        begin_at = taps_count - 1 - offset
        result = result + short_taps[offset][:, :, None] * padded[:, :, begin_at:begin_at + length]
    return result


def group_conv(operands):
    signal, kernel = operands
    fft_size = 2 * TOKENS
    spectrum = jnp.fft.rfft(signal.astype(jnp.float32), n=fft_size) * jnp.fft.rfft(kernel.astype(jnp.float32), n=fft_size)[None, :]
    return jnp.fft.irfft(spectrum, n=fft_size)[:, :TOKENS]


def reference(features, short_taps, filters, skip_gain, out_weight):
    conv_all = short_conv(features, short_taps)
    query_conv = conv_all[0]
    product = (conv_all[1] * conv_all[2]).astype(jnp.bfloat16)
    grouped = product.reshape(GROUPS, GROUP, TOKENS)
    longconv = lax.map(group_conv, (grouped, filters)).reshape(CH, TOKENS)
    long_mix = (longconv + skip_gain[:, None] * product.astype(jnp.float32)).astype(jnp.bfloat16)
    gated = (query_conv * long_mix.astype(jnp.float32)).astype(jnp.bfloat16)
    block_width = CH // N_TP
    summed = jnp.zeros((OUT, TOKENS), jnp.float32)
    for member in range(N_TP):
        weight_rows = out_weight[member * block_width:(member + 1) * block_width]
        gated_rows = gated[member * block_width:(member + 1) * block_width]
        partial_sum = jnp.dot(weight_rows.T, gated_rows, preferred_element_type=jnp.float32)
        rounded = lax.optimization_barrier(partial_sum.astype(jnp.bfloat16))
        summed = summed + rounded.astype(jnp.float32)
    return summed.astype(jnp.bfloat16)
```

```python
import functools
import math

import jax
import jax.numpy as jnp
from jax import lax
from jax.experimental import pallas as pl
from jax.experimental.pallas import tpu as pltpu
from jax.sharding import PartitionSpec as P

GROUP = 16


highest = lax.Precision.HIGHEST


def from_behind(value, axis, steps):
    count = lax.axis_size(axis)
    initial, last = (max(0, -steps), min(count, count - steps))
    return lax.ppermute(value, axis, [(source, source + steps) for source in range(initial, last)])


def left_product(matrix, stacked):
    return jnp.einsum("kn,bns->bks", matrix, stacked, precision=highest)


def right_product(stacked, matrix):
    return jnp.einsum("bks,st->bkt", stacked, matrix, precision=highest)


def split_length(total_len):
    row_count = 2
    for candidate in range(2, math.isqrt(total_len) + 1, 2):
        if total_len % candidate == 0:
            row_count = candidate
    return (row_count, total_len // row_count)


def dft_tables(row_count, col_count):
    total_len = row_count * col_count
    row_index = jnp.arange(row_count, dtype=jnp.int32)
    col_index = jnp.arange(col_count, dtype=jnp.int32)
    row_angle = (row_index[:, None] * row_index[None, :] % row_count).astype(jnp.float32) * (
        2.0 * math.pi / row_count
    )
    col_angle = (col_index[:, None] * col_index[None, :] % col_count).astype(jnp.float32) * (
        2.0 * math.pi / col_count
    )
    twist_angle = (row_index[:, None] * col_index[None, :] % total_len).astype(jnp.float32) * (
        2.0 * math.pi / total_len
    )
    return (
        jnp.cos(row_angle),
        jnp.sin(row_angle),
        jnp.cos(col_angle),
        jnp.sin(col_angle),
        jnp.cos(twist_angle),
        jnp.sin(twist_angle),
    )


def forward_dft(signal, tables):
    cos_row, sin_row, cos_col, sin_col, cos_twist, sin_twist = tables
    half_rows = signal.shape[1]
    first_real = left_product(cos_row[:, :half_rows], signal)
    first_imag = -left_product(sin_row[:, :half_rows], signal)
    twist_real = first_real * cos_twist + first_imag * sin_twist
    twist_imag = first_imag * cos_twist - first_real * sin_twist
    spec_real = right_product(twist_real, cos_col) + right_product(twist_imag, sin_col)
    spec_imag = right_product(twist_imag, cos_col) - right_product(twist_real, sin_col)
    return (spec_real, spec_imag)


def inverse_dft(spec_real, spec_imag, tables, half_rows):
    cos_row, sin_row, cos_col, sin_col, cos_twist, sin_twist = tables
    total_len = cos_row.shape[0] * cos_col.shape[0]
    middle_real = right_product(spec_real, cos_col) - right_product(spec_imag, sin_col)
    middle_imag = right_product(spec_imag, cos_col) + right_product(spec_real, sin_col)
    turned_real = middle_real * cos_twist - middle_imag * sin_twist
    turned_imag = middle_imag * cos_twist + middle_real * sin_twist
    signal = left_product(cos_row[:half_rows, :], turned_real) - left_product(
        sin_row[:half_rows, :], turned_imag
    )
    return signal / total_len


def local(features, short_taps, filters, skip_gain, out_weight):
    taps_count = short_taps.shape[0]
    chan_tp = features.shape[1]
    tok_local = features.shape[2]
    ctx_count = lax.axis_size("ctx")
    chan_dev = chan_tp // ctx_count
    group_dev = max(1, chan_dev // GROUP)
    per_group = chan_dev // group_dev
    seq_len = tok_local * ctx_count
    row_count, col_count = split_length(2 * seq_len)
    half_rows = row_count // 2
    tables = dft_tables(row_count, col_count)
    ctx_rank = lax.axis_index("ctx")
    kernel_rows = lax.dynamic_slice_in_dim(filters, ctx_rank * chan_dev // GROUP, group_dev, 0)
    kernel_real, kernel_imag = forward_dft(
        kernel_rows.astype(jnp.float32).reshape(group_dev, half_rows, col_count), tables
    )
    previous = from_behind(features[:, :, tok_local - (taps_count - 1) :], "ctx", 1)
    extended = jnp.concatenate([previous, features], axis=2).astype(jnp.float32)
    conv_all = jnp.zeros(features.shape, jnp.float32)
    for offset in range(taps_count):
        begin_at = taps_count - 1 - offset
        conv_all = (
            conv_all
            + short_taps[offset][:, :, None] * extended[:, :, begin_at : begin_at + tok_local]
        )
    query_conv = conv_all[0]
    product = (conv_all[1] * conv_all[2]).astype(jnp.bfloat16)
    gathered = lax.all_to_all(product, "ctx", split_axis=0, concat_axis=1, tiled=True)
    signal = gathered.astype(jnp.float32)
    sig_real, sig_imag = forward_dft(signal.reshape(chan_dev, half_rows, col_count), tables)
    four_shape = (group_dev, per_group, row_count, col_count)
    sig_real = sig_real.reshape(four_shape)
    sig_imag = sig_imag.reshape(four_shape)
    kernel_wide_real = kernel_real[:, None]
    kernel_wide_imag = kernel_imag[:, None]
    prod_real = (sig_real * kernel_wide_real - sig_imag * kernel_wide_imag).reshape(
        chan_dev, row_count, col_count
    )
    prod_imag = (sig_real * kernel_wide_imag + sig_imag * kernel_wide_real).reshape(
        chan_dev, row_count, col_count
    )
    longconv = inverse_dft(prod_real, prod_imag, tables, half_rows).reshape(chan_dev, seq_len)
    skip_local = lax.dynamic_slice_in_dim(skip_gain, ctx_rank * chan_dev, chan_dev, 0)
    long_mix = (longconv + skip_local[:, None] * signal).astype(jnp.bfloat16)
    restored = lax.all_to_all(long_mix, "ctx", split_axis=1, concat_axis=0, tiled=True)
    gated = (query_conv * restored.astype(jnp.float32)).astype(jnp.bfloat16)
    return lax.psum_scatter(
        lax.dot_general(
            out_weight, gated, (((0,), (0,)), ((), ())), preferred_element_type=jnp.float32
        ).astype(jnp.bfloat16),
        "tp",
        scatter_dimension=0,
        tiled=True,
    )


LANES = 128
NT = (((1,), (1,)), ((), ()))
NN = (((1,), (0,)), ((), ()))


def block_kernel(
    ctx_count, pieces, halves,
    features, short_taps, filters, skip_gain, weight_hbm, out,
    weight, weight_turned, taps_rows, taps, filters_wide, toeplitz,
    halo_tx, halo_rx, kv, kv_rx, mix_tx, mix_rx, query, gated,
    sib_tx, sib_rx, far_tx, far_rx,
    weight_sem, halo_send, halo_recv, kv_send, kv_recv, mix_send, mix_recv,
    sib_send, sib_recv, far_send, far_recv,
):
    taps_count = short_taps.shape[0]
    chan_tp, tok = features.shape[1:]
    chan_dev = chan_tp // ctx_count
    group_dev = chan_dev // GROUP
    out_dev = out.shape[0]
    me = lax.axis_index("ctx")
    rank = lax.axis_index("tp")
    core = lax.rem(rank, 2)
    sibling = rank + 1 - 2 * core
    far = lax.rem(rank + 2, 4)

    load_weight = pltpu.make_async_copy(weight_hbm, weight, weight_sem)
    load_weight.start()

    barrier = pltpu.get_barrier_semaphore()
    for step in range(1, ctx_count):
        pl.semaphore_signal(
            barrier, inc=1, device_id={"ctx": lax.rem(me + step, ctx_count)},
            device_id_type=pl.DeviceIdType.MESH,
        )
    for other in (sibling, far):
        pl.semaphore_signal(
            barrier, inc=1, device_id={"tp": other}, device_id_type=pl.DeviceIdType.MESH
        )

    halo_rows = halo_tx.shape[0]
    row_of = lax.broadcasted_iota(jnp.int32, (halo_rows, tok), 0)
    col_of = lax.broadcasted_iota(jnp.int32, (halo_rows, tok), 1)
    edge = jnp.zeros((halo_rows, chan_tp), jnp.float32)
    for row in range(3):
        pick = (row_of - row * (taps_count - 1) == col_of - (tok - taps_count + 1)) & (
            row_of >= row * (taps_count - 1)
        ) & (row_of < (row + 1) * (taps_count - 1))
        edge += lax.dot_general(
            pick.astype(jnp.bfloat16), features[row], NT, preferred_element_type=jnp.float32
        )
    halo_tx[...] = edge.astype(jnp.bfloat16)

    pl.semaphore_wait(barrier, ctx_count + 1)

    def halo_copy():
        return pltpu.make_async_remote_copy(
            src_ref=halo_tx, dst_ref=halo_rx, send_sem=halo_send, recv_sem=halo_recv,
            device_id={"ctx": lax.rem(me + 1, ctx_count)},
            device_id_type=pl.DeviceIdType.MESH,
        )

    @pl.when(me < ctx_count - 1)
    def _():
        halo_copy().start()

    taps_rows[...] = jnp.zeros_like(taps_rows)
    for offset in range(taps_count):
        taps_rows[3 * offset : 3 * offset + 3, :] = short_taps[offset]
    taps_rows[3 * taps_count : 3 * taps_count + 1, :] = skip_gain[...]
    taps[...] = taps_rows[...].T

    @pl.when(me > 0)
    def _():
        halo_copy().wait_recv()

    @pl.when(me == 0)
    def _():
        halo_rx[...] = jnp.zeros_like(halo_rx)

    halo = halo_rx[...].astype(jnp.float32).T
    lane = lax.broadcasted_iota(jnp.int32, (chan_tp, tok), 1)

    def short_conv(row):
        values = features[row].astype(jnp.float32)
        total = taps[:, row : row + 1] * values
        for offset in range(1, taps_count):
            moved = pltpu.roll(values, offset, 1)
            for place in range(offset):
                column = row * (taps_count - 1) + taps_count - 1 - offset + place
                moved = jnp.where(lane == place, halo[:, column : column + 1], moved)
            index = 3 * offset + row
            total = total + taps[:, index : index + 1] * moved
        return total

    kv[...] = (short_conv(1) * short_conv(2)).astype(jnp.bfloat16)

    part = chan_dev // pieces

    def kv_copy(step, piece):
        target = lax.rem(me + step, ctx_count)
        begin = pl.multiple_of(target * chan_dev + piece * part, part)
        return pltpu.make_async_remote_copy(
            src_ref=kv.at[pl.ds(begin, part)],
            dst_ref=kv_rx.at[me, pl.ds(piece * part, part)],
            send_sem=kv_send.at[piece, step], recv_sem=kv_recv.at[piece, step],
            device_id={"ctx": target}, device_id_type=pl.DeviceIdType.MESH,
        )

    def mix_copy(step, piece):
        target = lax.rem(me + step, ctx_count)
        begin = pl.multiple_of(me * chan_dev + piece * part, part)
        return pltpu.make_async_remote_copy(
            src_ref=mix_tx.at[target, pl.ds(piece * part, part)],
            dst_ref=mix_rx.at[pl.ds(begin, part)],
            send_sem=mix_send.at[piece, step], recv_sem=mix_recv.at[piece, step],
            device_id={"ctx": target}, device_id_type=pl.DeviceIdType.MESH,
        )

    order = sorted(range(1, ctx_count), key=lambda step: -min(step, ctx_count - step))
    for piece in range(pieces):
        for step in order:
            kv_copy(step, piece).start()
    own = pl.ds(pl.multiple_of(me * chan_dev, chan_dev), chan_dev)
    kv_rx[me] = kv[own, :]

    filters_wide[...] = filters[...].astype(jnp.float32)
    length = filters.shape[1]
    wide_row = lax.broadcasted_iota(jnp.int32, (tok, length), 0)
    wide_col = lax.broadcasted_iota(jnp.int32, (tok, length), 1)
    for group in range(group_dev):
        taps_long = filters_wide[pl.ds(me * group_dev + group, 1), :]
        spread = pltpu.roll(
            jnp.broadcast_to(taps_long, (tok, length)), 0, 1, stride=1, stride_axis=0
        )
        toeplitz[group] = jnp.where(wide_col >= wide_row, spread, 0.0).astype(jnp.bfloat16)
    query[...] = short_conv(0)
    load_weight.wait()
    turn = 256

    @pl.loop(0, weight.shape[1] // turn)
    def _(index):
        begin = pl.multiple_of(index * turn, turn)
        weight_turned[pl.ds(begin, turn), :] = weight[:, pl.ds(begin, turn)].T

    groups_part = group_dev // pieces
    for piece in range(pieces):
        for step in order:
            kv_copy(step, piece).wait_recv()
        for group in range(piece * groups_part, (piece + 1) * groups_part):
            rows = slice(group * GROUP, (group + 1) * GROUP)
            signal = kv_rx[:, rows, :].reshape(ctx_count * GROUP, tok)
            begin = pl.multiple_of(me * chan_dev + group * GROUP, GROUP)
            column = 3 * taps_count
            direct = taps[pl.ds(begin, GROUP), :][:, column : column + 1]
            totals = [
                direct * kv_rx[block, rows, :].astype(jnp.float32) for block in range(ctx_count)
            ]
            wide = 2 if ctx_count % 2 == 0 else 1
            for distance in range(0, ctx_count, wide):
                products = lax.dot_general(
                    signal[: (ctx_count - distance) * GROUP],
                    toeplitz[group, :, distance * tok : (distance + wide) * tok],
                    NN, preferred_element_type=jnp.float32,
                )
                for more in range(wide):
                    for block in range(distance + more, ctx_count):
                        source = block - distance - more
                        totals[block] += products[
                            source * GROUP : (source + 1) * GROUP, more * tok : (more + 1) * tok
                        ]
            for block in range(ctx_count):
                mix_tx[block, rows, :] = totals[block].astype(jnp.bfloat16)
        for step in order:
            mix_copy(step, piece).start()
    mix_rx[own, :] = mix_tx[me]

    for piece in range(pieces):
        for step in order:
            mix_copy(step, piece).wait_recv()
    gated[...] = (query[...] * mix_rx[...].astype(jnp.float32)).astype(jnp.bfloat16)

    rows_half = out_dev // halves

    def partial(owner, half):
        begin = pl.multiple_of(owner * out_dev + half * rows_half, rows_half)
        return lax.dot_general(
            weight_turned[pl.ds(begin, rows_half), :], gated[...], NN,
            preferred_element_type=jnp.float32,
        )

    def half_of(half):
        return pl.ds(half * rows_half, rows_half)

    def sib_copy(slot, half):
        return pltpu.make_async_remote_copy(
            src_ref=sib_tx.at[slot, half_of(half)], dst_ref=sib_rx.at[slot, half_of(half)],
            send_sem=sib_send.at[slot, half], recv_sem=sib_recv.at[slot, half],
            device_id={"tp": sibling}, device_id_type=pl.DeviceIdType.MESH,
        )

    def far_copy(half):
        return pltpu.make_async_remote_copy(
            src_ref=far_tx.at[half_of(half)], dst_ref=far_rx.at[half_of(half)],
            send_sem=far_send.at[half], recv_sem=far_recv.at[half],
            device_id={"tp": far}, device_id_type=pl.DeviceIdType.MESH,
        )

    far_sibling = lax.rem(sibling + 2, 4)
    for half in range(halves):
        sib_tx[0, half_of(half), :] = partial(far_sibling, half).astype(jnp.bfloat16)
        sib_copy(0, half).start()
    for half in range(halves):
        mine = partial(far, half)
        sib_copy(0, half).wait_recv()
        far_tx[half_of(half), :] = (
            mine + sib_rx[0, half_of(half), :].astype(jnp.float32)
        ).astype(jnp.bfloat16)
        far_copy(half).start()
    for half in range(halves):
        sib_tx[1, half_of(half), :] = partial(sibling, half).astype(jnp.bfloat16)
        sib_copy(1, half).start()
    for half in range(halves):
        mine = partial(rank, half)
        sib_copy(1, half).wait_recv()
        mine += sib_rx[1, half_of(half), :].astype(jnp.float32)
        far_copy(half).wait_recv()
        out[half_of(half), :] = (
            mine + far_rx[half_of(half), :].astype(jnp.float32)
        ).astype(jnp.bfloat16)

    @pl.when(me < ctx_count - 1)
    def _():
        halo_copy().wait_send()

    for piece in range(pieces):
        for step in order:
            kv_copy(step, piece).wait_send()
            mix_copy(step, piece).wait_send()
    for half in range(halves):
        sib_copy(0, half).wait_send()
        sib_copy(1, half).wait_send()
        far_copy(half).wait_send()


def fused(features, short_taps, filters, skip_gain, out_weight):
    taps_count = short_taps.shape[0]
    _, chan_tp, tok = features.shape
    ctx_count = lax.axis_size("ctx")
    group_rows, length = filters.shape
    chan_dev = chan_tp // ctx_count
    group_dev = chan_dev // GROUP
    out_all = out_weight.shape[1]
    out_dev = out_all // lax.axis_size("tp")
    pieces = 2 if group_dev % 2 == 0 else 1
    halves = 2
    bf16, f32 = jnp.bfloat16, jnp.float32
    vmem = pl.BlockSpec(memory_space=pltpu.VMEM)
    dma = pltpu.SemaphoreType.DMA
    return pl.pallas_call(
        functools.partial(block_kernel, ctx_count, pieces, halves),
        out_shape=jax.ShapeDtypeStruct((out_dev, tok), bf16),
        in_specs=[vmem] * 4 + [pl.BlockSpec(memory_space=pl.ANY)],
        out_specs=vmem,
        scratch_shapes=[
            pltpu.VMEM((chan_tp, out_all), bf16),
            pltpu.VMEM((out_all, chan_tp), bf16),
            pltpu.VMEM((16, chan_tp), f32),
            pltpu.VMEM((chan_tp, 16), f32),
            pltpu.VMEM((group_rows, length), f32),
            pltpu.VMEM((group_dev, tok, length), bf16),
            pltpu.VMEM((16, chan_tp), bf16),
            pltpu.VMEM((16, chan_tp), bf16),
            pltpu.VMEM((chan_tp, tok), bf16),
            pltpu.VMEM((ctx_count, chan_dev, tok), bf16),
            pltpu.VMEM((ctx_count, chan_dev, tok), bf16),
            pltpu.VMEM((chan_tp, tok), bf16),
            pltpu.VMEM((chan_tp, tok), f32),
            pltpu.VMEM((chan_tp, tok), bf16),
            pltpu.VMEM((2, out_dev, tok), bf16),
            pltpu.VMEM((2, out_dev, tok), bf16),
            pltpu.VMEM((out_dev, tok), bf16),
            pltpu.VMEM((out_dev, tok), bf16),
            dma, dma, dma,
            dma((pieces, ctx_count)), dma((pieces, ctx_count)),
            dma((pieces, ctx_count)), dma((pieces, ctx_count)),
            dma((2, halves)), dma((2, halves)),
            dma((halves,)), dma((halves,)),
        ],
        compiler_params=pltpu.CompilerParams(
            collective_id=0, has_side_effects=True, vmem_limit_bytes=40 * 2**20
        ),
    )(features, short_taps, filters, skip_gain.reshape(1, chan_tp), out_weight)


def fits_kernel(mesh, features, short_taps, filters, skip_gain, out_weight):
    ctx_count, tp_count = mesh.shape["ctx"], mesh.shape["tp"]
    rows, channels, tokens = features.shape
    taps_count = short_taps.shape[0]
    tok = tokens // ctx_count
    chan_tp = channels // tp_count
    toeplitz_bytes = chan_tp // ctx_count // GROUP * tok * tokens * 2
    return (
        tp_count == 4
        and tok == LANES
        and rows * (taps_count - 1) <= 16
        and rows * taps_count < 16
        and chan_tp % (ctx_count * GROUP) == 0
        and chan_tp % LANES == 0
        and out_weight.shape[1] % (tp_count * 256) == 0
        and toeplitz_bytes <= 2**22
    )


def solution(mesh):
    placed = (P(None, "tp", "ctx"), P(None, None, "tp"), P("tp", None), P("tp"), P("tp", None))

    def run(*arrays):
        body = fused if fits_kernel(mesh, *arrays) else local
        return jax.shard_map(
            body, mesh=mesh, in_specs=placed, out_specs=P("tp", "ctx"), check_vma=False
        )(*arrays)

    return run
```

```python
import functools
import math

import jax
import jax.numpy as jnp
from jax import lax
from jax.experimental import pallas as pl
from jax.experimental.pallas import tpu as pltpu
from jax.sharding import PartitionSpec as P

GROUP = 16


highest = lax.Precision.HIGHEST


def from_behind(value, axis, steps):
    count = lax.axis_size(axis)
    initial, last = (max(0, -steps), min(count, count - steps))
    return lax.ppermute(value, axis, [(source, source + steps) for source in range(initial, last)])


def left_product(matrix, stacked):
    return jnp.einsum("kn,bns->bks", matrix, stacked, precision=highest)


def right_product(stacked, matrix):
    return jnp.einsum("bks,st->bkt", stacked, matrix, precision=highest)


def split_length(total_len):
    row_count = 2
    for candidate in range(2, math.isqrt(total_len) + 1, 2):
        if total_len % candidate == 0:
            row_count = candidate
    return (row_count, total_len // row_count)


def dft_tables(row_count, col_count):
    total_len = row_count * col_count
    row_index = jnp.arange(row_count, dtype=jnp.int32)
    col_index = jnp.arange(col_count, dtype=jnp.int32)
    row_angle = (row_index[:, None] * row_index[None, :] % row_count).astype(jnp.float32) * (
        2.0 * math.pi / row_count
    )
    col_angle = (col_index[:, None] * col_index[None, :] % col_count).astype(jnp.float32) * (
        2.0 * math.pi / col_count
    )
    twist_angle = (row_index[:, None] * col_index[None, :] % total_len).astype(jnp.float32) * (
        2.0 * math.pi / total_len
    )
    return (
        jnp.cos(row_angle),
        jnp.sin(row_angle),
        jnp.cos(col_angle),
        jnp.sin(col_angle),
        jnp.cos(twist_angle),
        jnp.sin(twist_angle),
    )


def forward_dft(signal, tables):
    cos_row, sin_row, cos_col, sin_col, cos_twist, sin_twist = tables
    half_rows = signal.shape[1]
    first_real = left_product(cos_row[:, :half_rows], signal)
    first_imag = -left_product(sin_row[:, :half_rows], signal)
    twist_real = first_real * cos_twist + first_imag * sin_twist
    twist_imag = first_imag * cos_twist - first_real * sin_twist
    spec_real = right_product(twist_real, cos_col) + right_product(twist_imag, sin_col)
    spec_imag = right_product(twist_imag, cos_col) - right_product(twist_real, sin_col)
    return (spec_real, spec_imag)


def inverse_dft(spec_real, spec_imag, tables, half_rows):
    cos_row, sin_row, cos_col, sin_col, cos_twist, sin_twist = tables
    total_len = cos_row.shape[0] * cos_col.shape[0]
    middle_real = right_product(spec_real, cos_col) - right_product(spec_imag, sin_col)
    middle_imag = right_product(spec_imag, cos_col) + right_product(spec_real, sin_col)
    turned_real = middle_real * cos_twist - middle_imag * sin_twist
    turned_imag = middle_imag * cos_twist + middle_real * sin_twist
    signal = left_product(cos_row[:half_rows, :], turned_real) - left_product(
        sin_row[:half_rows, :], turned_imag
    )
    return signal / total_len


def local(features, short_taps, filters, skip_gain, out_weight):
    taps_count = short_taps.shape[0]
    chan_tp = features.shape[1]
    tok_local = features.shape[2]
    ctx_count = lax.axis_size("ctx")
    chan_dev = chan_tp // ctx_count
    group_dev = max(1, chan_dev // GROUP)
    per_group = chan_dev // group_dev
    seq_len = tok_local * ctx_count
    row_count, col_count = split_length(2 * seq_len)
    half_rows = row_count // 2
    tables = dft_tables(row_count, col_count)
    ctx_rank = lax.axis_index("ctx")
    kernel_rows = lax.dynamic_slice_in_dim(filters, ctx_rank * chan_dev // GROUP, group_dev, 0)
    kernel_real, kernel_imag = forward_dft(
        kernel_rows.astype(jnp.float32).reshape(group_dev, half_rows, col_count), tables
    )
    previous = from_behind(features[:, :, tok_local - (taps_count - 1) :], "ctx", 1)
    extended = jnp.concatenate([previous, features], axis=2).astype(jnp.float32)
    conv_all = jnp.zeros(features.shape, jnp.float32)
    for offset in range(taps_count):
        begin_at = taps_count - 1 - offset
        conv_all = (
            conv_all
            + short_taps[offset][:, :, None] * extended[:, :, begin_at : begin_at + tok_local]
        )
    query_conv = conv_all[0]
    product = (conv_all[1] * conv_all[2]).astype(jnp.bfloat16)
    gathered = lax.all_to_all(product, "ctx", split_axis=0, concat_axis=1, tiled=True)
    signal = gathered.astype(jnp.float32)
    sig_real, sig_imag = forward_dft(signal.reshape(chan_dev, half_rows, col_count), tables)
    four_shape = (group_dev, per_group, row_count, col_count)
    sig_real = sig_real.reshape(four_shape)
    sig_imag = sig_imag.reshape(four_shape)
    kernel_wide_real = kernel_real[:, None]
    kernel_wide_imag = kernel_imag[:, None]
    prod_real = (sig_real * kernel_wide_real - sig_imag * kernel_wide_imag).reshape(
        chan_dev, row_count, col_count
    )
    prod_imag = (sig_real * kernel_wide_imag + sig_imag * kernel_wide_real).reshape(
        chan_dev, row_count, col_count
    )
    longconv = inverse_dft(prod_real, prod_imag, tables, half_rows).reshape(chan_dev, seq_len)
    skip_local = lax.dynamic_slice_in_dim(skip_gain, ctx_rank * chan_dev, chan_dev, 0)
    long_mix = (longconv + skip_local[:, None] * signal).astype(jnp.bfloat16)
    restored = lax.all_to_all(long_mix, "ctx", split_axis=1, concat_axis=0, tiled=True)
    gated = (query_conv * restored.astype(jnp.float32)).astype(jnp.bfloat16)
    return lax.psum_scatter(
        lax.dot_general(
            out_weight, gated, (((0,), (0,)), ((), ())), preferred_element_type=jnp.float32
        ).astype(jnp.bfloat16),
        "tp",
        scatter_dimension=0,
        tiled=True,
    )


LANES = 128
NT = (((1,), (1,)), ((), ()))
NN = (((1,), (0,)), ((), ()))


def block_kernel(
    ctx_count, pieces, halves,
    features_hbm, short_taps_hbm, filters_hbm, skip_gain_hbm, weight_hbm, out,
    features, short_taps, filters, skip_gain, weight, weight_turned, taps_rows, taps, filters_wide, toeplitz,
    halo_tx, halo_rx, kv, kv_rx, mix_tx, mix_rx, query, gated,
    sib_tx, sib_rx, far_tx, far_rx,
    load_sem, halo_send, halo_recv, kv_send, kv_recv, mix_send, mix_recv,
    sib_send, sib_recv, far_send, far_recv,
):
    loads = [
        pltpu.make_async_copy(source, target, load_sem.at[index])
        for index, (source, target) in enumerate((
            (features_hbm, features), (short_taps_hbm, short_taps), (skip_gain_hbm, skip_gain),
            (filters_hbm, filters), (weight_hbm, weight),
        ))
    ]
    for load in loads:
        load.start()
    taps_count = short_taps.shape[0]
    chan_tp, tok = features.shape[1:]
    chan_dev = chan_tp // ctx_count
    group_dev = chan_dev // GROUP
    out_dev = out.shape[0]
    me = lax.axis_index("ctx")
    rank = lax.axis_index("tp")
    core = lax.rem(rank, 2)
    sibling = rank + 1 - 2 * core
    far = lax.rem(rank + 2, 4)

    barrier = pltpu.get_barrier_semaphore()
    for step in range(1, ctx_count):
        pl.semaphore_signal(
            barrier, inc=1, device_id={"ctx": lax.rem(me + step, ctx_count)},
            device_id_type=pl.DeviceIdType.MESH,
        )
    for other in (sibling, far):
        pl.semaphore_signal(
            barrier, inc=1, device_id={"tp": other}, device_id_type=pl.DeviceIdType.MESH
        )

    halo_rows = halo_tx.shape[0]
    row_of = lax.broadcasted_iota(jnp.int32, (halo_rows, tok), 0)
    col_of = lax.broadcasted_iota(jnp.int32, (halo_rows, tok), 1)
    loads[0].wait()
    edge = jnp.zeros((halo_rows, chan_tp), jnp.float32)
    for row in range(3):
        pick = (row_of - row * (taps_count - 1) == col_of - (tok - taps_count + 1)) & (
            row_of >= row * (taps_count - 1)
        ) & (row_of < (row + 1) * (taps_count - 1))
        edge += lax.dot_general(
            pick.astype(jnp.bfloat16), features[row], NT, preferred_element_type=jnp.float32
        )
    halo_tx[...] = edge.astype(jnp.bfloat16)

    pl.semaphore_wait(barrier, ctx_count + 1)

    def halo_copy():
        return pltpu.make_async_remote_copy(
            src_ref=halo_tx, dst_ref=halo_rx, send_sem=halo_send, recv_sem=halo_recv,
            device_id={"ctx": lax.rem(me + 1, ctx_count)},
            device_id_type=pl.DeviceIdType.MESH,
        )

    @pl.when(me < ctx_count - 1)
    def _():
        halo_copy().start()

    taps_rows[...] = jnp.zeros_like(taps_rows)
    loads[1].wait()
    loads[2].wait()
    for offset in range(taps_count):
        taps_rows[3 * offset : 3 * offset + 3, :] = short_taps[offset]
    taps_rows[3 * taps_count : 3 * taps_count + 1, :] = skip_gain[...]
    taps[...] = taps_rows[...].T

    @pl.when(me > 0)
    def _():
        halo_copy().wait_recv()

    @pl.when(me == 0)
    def _():
        halo_rx[...] = jnp.zeros_like(halo_rx)

    halo = halo_rx[...].astype(jnp.float32).T
    lane = lax.broadcasted_iota(jnp.int32, (chan_tp, tok), 1)

    def short_conv(row):
        values = features[row].astype(jnp.float32)
        total = taps[:, row : row + 1] * values
        for offset in range(1, taps_count):
            moved = pltpu.roll(values, offset, 1)
            for place in range(offset):
                column = row * (taps_count - 1) + taps_count - 1 - offset + place
                moved = jnp.where(lane == place, halo[:, column : column + 1], moved)
            index = 3 * offset + row
            total = total + taps[:, index : index + 1] * moved
        return total

    kv[...] = (short_conv(1) * short_conv(2)).astype(jnp.bfloat16)

    part = chan_dev // pieces

    def kv_copy(step, piece):
        target = lax.rem(me + step, ctx_count)
        begin = pl.multiple_of(target * chan_dev + piece * part, part)
        return pltpu.make_async_remote_copy(
            src_ref=kv.at[pl.ds(begin, part)],
            dst_ref=kv_rx.at[me, pl.ds(piece * part, part)],
            send_sem=kv_send.at[piece, step], recv_sem=kv_recv.at[piece, step],
            device_id={"ctx": target}, device_id_type=pl.DeviceIdType.MESH,
        )

    def mix_copy(step, piece):
        target = lax.rem(me + step, ctx_count)
        begin = pl.multiple_of(me * chan_dev + piece * part, part)
        return pltpu.make_async_remote_copy(
            src_ref=mix_tx.at[target, pl.ds(piece * part, part)],
            dst_ref=mix_rx.at[pl.ds(begin, part)],
            send_sem=mix_send.at[piece, step], recv_sem=mix_recv.at[piece, step],
            device_id={"ctx": target}, device_id_type=pl.DeviceIdType.MESH,
        )

    order = sorted(range(1, ctx_count), key=lambda step: -min(step, ctx_count - step))
    for piece in range(pieces):
        for step in order:
            kv_copy(step, piece).start()
    own = pl.ds(pl.multiple_of(me * chan_dev, chan_dev), chan_dev)
    kv_rx[me] = kv[own, :]

    loads[3].wait()
    filters_wide[...] = filters[...].astype(jnp.float32)
    length = filters.shape[1]
    wide_row = lax.broadcasted_iota(jnp.int32, (tok, length), 0)
    wide_col = lax.broadcasted_iota(jnp.int32, (tok, length), 1)
    for group in range(group_dev):
        taps_long = filters_wide[pl.ds(me * group_dev + group, 1), :]
        spread = pltpu.roll(
            jnp.broadcast_to(taps_long, (tok, length)), 0, 1, stride=1, stride_axis=0
        )
        toeplitz[group] = jnp.where(wide_col >= wide_row, spread, 0.0).astype(jnp.bfloat16)
    query[...] = short_conv(0)
    groups_part = group_dev // pieces
    for piece in range(pieces):
        for step in order:
            kv_copy(step, piece).wait_recv()
        for group in range(piece * groups_part, (piece + 1) * groups_part):
            rows = slice(group * GROUP, (group + 1) * GROUP)
            signal = kv_rx[:, rows, :].reshape(ctx_count * GROUP, tok)
            begin = pl.multiple_of(me * chan_dev + group * GROUP, GROUP)
            column = 3 * taps_count
            direct = taps[pl.ds(begin, GROUP), :][:, column : column + 1]
            totals = [
                direct * kv_rx[block, rows, :].astype(jnp.float32) for block in range(ctx_count)
            ]
            wide = 2 if ctx_count % 2 == 0 else 1
            for distance in range(0, ctx_count, wide):
                products = lax.dot_general(
                    signal[: (ctx_count - distance) * GROUP],
                    toeplitz[group, :, distance * tok : (distance + wide) * tok],
                    NN, preferred_element_type=jnp.float32,
                )
                for more in range(wide):
                    for block in range(distance + more, ctx_count):
                        source = block - distance - more
                        totals[block] += products[
                            source * GROUP : (source + 1) * GROUP, more * tok : (more + 1) * tok
                        ]
            for block in range(ctx_count):
                mix_tx[block, rows, :] = totals[block].astype(jnp.bfloat16)
        for step in order:
            mix_copy(step, piece).start()
    mix_rx[own, :] = mix_tx[me]
    loads[4].wait()
    turn = 256

    @pl.loop(0, weight.shape[1] // turn)
    def _(index):
        begin = pl.multiple_of(index * turn, turn)
        weight_turned[pl.ds(begin, turn), :] = weight[:, pl.ds(begin, turn)].T

    for piece in range(pieces):
        for step in order:
            mix_copy(step, piece).wait_recv()
    gated[...] = (query[...] * mix_rx[...].astype(jnp.float32)).astype(jnp.bfloat16)

    rows_half = out_dev // halves

    def partial(owner, half):
        begin = pl.multiple_of(owner * out_dev + half * rows_half, rows_half)
        return lax.dot_general(
            weight_turned[pl.ds(begin, rows_half), :], gated[...], NN,
            preferred_element_type=jnp.float32,
        )

    def half_of(half):
        return pl.ds(half * rows_half, rows_half)

    def sib_copy(slot, half):
        return pltpu.make_async_remote_copy(
            src_ref=sib_tx.at[slot, half_of(half)], dst_ref=sib_rx.at[slot, half_of(half)],
            send_sem=sib_send.at[slot, half], recv_sem=sib_recv.at[slot, half],
            device_id={"tp": sibling}, device_id_type=pl.DeviceIdType.MESH,
        )

    def far_copy(half):
        return pltpu.make_async_remote_copy(
            src_ref=far_tx.at[half_of(half)], dst_ref=far_rx.at[half_of(half)],
            send_sem=far_send.at[half], recv_sem=far_recv.at[half],
            device_id={"tp": far}, device_id_type=pl.DeviceIdType.MESH,
        )

    far_sibling = lax.rem(sibling + 2, 4)
    for half in range(halves):
        sib_tx[0, half_of(half), :] = partial(far_sibling, half).astype(jnp.bfloat16)
        sib_copy(0, half).start()
    for half in range(halves):
        mine = partial(far, half)
        sib_copy(0, half).wait_recv()
        far_tx[half_of(half), :] = (
            mine + sib_rx[0, half_of(half), :].astype(jnp.float32)
        ).astype(jnp.bfloat16)
        far_copy(half).start()
    for half in range(halves):
        sib_tx[1, half_of(half), :] = partial(sibling, half).astype(jnp.bfloat16)
        sib_copy(1, half).start()
    for half in range(halves):
        mine = partial(rank, half)
        sib_copy(1, half).wait_recv()
        mine += sib_rx[1, half_of(half), :].astype(jnp.float32)
        far_copy(half).wait_recv()
        out[half_of(half), :] = (
            mine + far_rx[half_of(half), :].astype(jnp.float32)
        ).astype(jnp.bfloat16)

    @pl.when(me < ctx_count - 1)
    def _():
        halo_copy().wait_send()

    for piece in range(pieces):
        for step in order:
            kv_copy(step, piece).wait_send()
            mix_copy(step, piece).wait_send()
    for half in range(halves):
        sib_copy(0, half).wait_send()
        sib_copy(1, half).wait_send()
        far_copy(half).wait_send()


def fused(features, short_taps, filters, skip_gain, out_weight):
    taps_count = short_taps.shape[0]
    _, chan_tp, tok = features.shape
    ctx_count = lax.axis_size("ctx")
    group_rows, length = filters.shape
    chan_dev = chan_tp // ctx_count
    group_dev = chan_dev // GROUP
    out_all = out_weight.shape[1]
    out_dev = out_all // lax.axis_size("tp")
    pieces = 2 if group_dev % 2 == 0 else 1
    halves = 2
    bf16, f32 = jnp.bfloat16, jnp.float32
    dma = pltpu.SemaphoreType.DMA
    return pl.pallas_call(
        functools.partial(block_kernel, ctx_count, pieces, halves),
        out_shape=jax.ShapeDtypeStruct((out_dev, tok), bf16),
        in_specs=[pl.BlockSpec(memory_space=pltpu.HBM)] * 5,
        out_specs=pl.BlockSpec(memory_space=pltpu.VMEM),
        scratch_shapes=[
            pltpu.VMEM(features.shape, bf16),
            pltpu.VMEM(short_taps.shape, f32),
            pltpu.VMEM(filters.shape, bf16),
            pltpu.VMEM((1, chan_tp), f32),
            pltpu.VMEM((chan_tp, out_all), bf16),
            pltpu.VMEM((out_all, chan_tp), bf16),
            pltpu.VMEM((16, chan_tp), f32),
            pltpu.VMEM((chan_tp, 16), f32),
            pltpu.VMEM((group_rows, length), f32),
            pltpu.VMEM((group_dev, tok, length), bf16),
            pltpu.VMEM((16, chan_tp), bf16),
            pltpu.VMEM((16, chan_tp), bf16),
            pltpu.VMEM((chan_tp, tok), bf16),
            pltpu.VMEM((ctx_count, chan_dev, tok), bf16),
            pltpu.VMEM((ctx_count, chan_dev, tok), bf16),
            pltpu.VMEM((chan_tp, tok), bf16),
            pltpu.VMEM((chan_tp, tok), f32),
            pltpu.VMEM((chan_tp, tok), bf16),
            pltpu.VMEM((2, out_dev, tok), bf16),
            pltpu.VMEM((2, out_dev, tok), bf16),
            pltpu.VMEM((out_dev, tok), bf16),
            pltpu.VMEM((out_dev, tok), bf16),
            dma((5,)), dma, dma,
            dma((pieces, ctx_count)), dma((pieces, ctx_count)),
            dma((pieces, ctx_count)), dma((pieces, ctx_count)),
            dma((2, halves)), dma((2, halves)),
            dma((halves,)), dma((halves,)),
        ],
        compiler_params=pltpu.CompilerParams(
            collective_id=0, has_side_effects=True, vmem_limit_bytes=62 * 2**20
        ),
    )(features, short_taps, filters, skip_gain.reshape(1, chan_tp), out_weight)


def fits_kernel(mesh, features, short_taps, filters, skip_gain, out_weight):
    ctx_count, tp_count = mesh.shape["ctx"], mesh.shape["tp"]
    rows, channels, tokens = features.shape
    taps_count = short_taps.shape[0]
    tok = tokens // ctx_count
    chan_tp = channels // tp_count
    toeplitz_bytes = chan_tp // ctx_count // GROUP * tok * tokens * 2
    return (
        tp_count == 4
        and tok == LANES
        and rows * (taps_count - 1) <= 16
        and rows * taps_count < 16
        and chan_tp % (ctx_count * GROUP) == 0
        and chan_tp % LANES == 0
        and out_weight.shape[1] % (tp_count * 256) == 0
        and toeplitz_bytes <= 2**22
    )


def solution(mesh):
    placed = (P(None, "tp", "ctx"), P(None, None, "tp"), P("tp", None), P("tp"), P("tp", None))

    def run(*arrays):
        body = fused if fits_kernel(mesh, *arrays) else local
        return jax.shard_map(
            body, mesh=mesh, in_specs=placed, out_specs=P("tp", "ctx"), check_vma=False
        )(*arrays)

    return run
```

```python
import functools
import math

import jax
import jax.numpy as jnp
from jax import lax
from jax.experimental import pallas as pl
from jax.experimental.pallas import tpu as pltpu
from jax.sharding import PartitionSpec as P

GROUP = 16


highest = lax.Precision.HIGHEST


def from_behind(value, axis, steps):
    count = lax.axis_size(axis)
    initial, last = (max(0, -steps), min(count, count - steps))
    return lax.ppermute(value, axis, [(source, source + steps) for source in range(initial, last)])


def left_product(matrix, stacked):
    return jnp.einsum("kn,bns->bks", matrix, stacked, precision=highest)


def right_product(stacked, matrix):
    return jnp.einsum("bks,st->bkt", stacked, matrix, precision=highest)


def split_length(total_len):
    row_count = 2
    for candidate in range(2, math.isqrt(total_len) + 1, 2):
        if total_len % candidate == 0:
            row_count = candidate
    return (row_count, total_len // row_count)


def dft_tables(row_count, col_count):
    total_len = row_count * col_count
    row_index = jnp.arange(row_count, dtype=jnp.int32)
    col_index = jnp.arange(col_count, dtype=jnp.int32)
    row_angle = (row_index[:, None] * row_index[None, :] % row_count).astype(jnp.float32) * (
        2.0 * math.pi / row_count
    )
    col_angle = (col_index[:, None] * col_index[None, :] % col_count).astype(jnp.float32) * (
        2.0 * math.pi / col_count
    )
    twist_angle = (row_index[:, None] * col_index[None, :] % total_len).astype(jnp.float32) * (
        2.0 * math.pi / total_len
    )
    return (
        jnp.cos(row_angle),
        jnp.sin(row_angle),
        jnp.cos(col_angle),
        jnp.sin(col_angle),
        jnp.cos(twist_angle),
        jnp.sin(twist_angle),
    )


def forward_dft(signal, tables):
    cos_row, sin_row, cos_col, sin_col, cos_twist, sin_twist = tables
    half_rows = signal.shape[1]
    first_real = left_product(cos_row[:, :half_rows], signal)
    first_imag = -left_product(sin_row[:, :half_rows], signal)
    twist_real = first_real * cos_twist + first_imag * sin_twist
    twist_imag = first_imag * cos_twist - first_real * sin_twist
    spec_real = right_product(twist_real, cos_col) + right_product(twist_imag, sin_col)
    spec_imag = right_product(twist_imag, cos_col) - right_product(twist_real, sin_col)
    return (spec_real, spec_imag)


def inverse_dft(spec_real, spec_imag, tables, half_rows):
    cos_row, sin_row, cos_col, sin_col, cos_twist, sin_twist = tables
    total_len = cos_row.shape[0] * cos_col.shape[0]
    middle_real = right_product(spec_real, cos_col) - right_product(spec_imag, sin_col)
    middle_imag = right_product(spec_imag, cos_col) + right_product(spec_real, sin_col)
    turned_real = middle_real * cos_twist - middle_imag * sin_twist
    turned_imag = middle_imag * cos_twist + middle_real * sin_twist
    signal = left_product(cos_row[:half_rows, :], turned_real) - left_product(
        sin_row[:half_rows, :], turned_imag
    )
    return signal / total_len


def local(features, short_taps, filters, skip_gain, out_weight):
    taps_count = short_taps.shape[0]
    chan_tp = features.shape[1]
    tok_local = features.shape[2]
    ctx_count = lax.axis_size("ctx")
    chan_dev = chan_tp // ctx_count
    group_dev = max(1, chan_dev // GROUP)
    per_group = chan_dev // group_dev
    seq_len = tok_local * ctx_count
    row_count, col_count = split_length(2 * seq_len)
    half_rows = row_count // 2
    tables = dft_tables(row_count, col_count)
    ctx_rank = lax.axis_index("ctx")
    kernel_rows = lax.dynamic_slice_in_dim(filters, ctx_rank * chan_dev // GROUP, group_dev, 0)
    kernel_real, kernel_imag = forward_dft(
        kernel_rows.astype(jnp.float32).reshape(group_dev, half_rows, col_count), tables
    )
    previous = from_behind(features[:, :, tok_local - (taps_count - 1) :], "ctx", 1)
    extended = jnp.concatenate([previous, features], axis=2).astype(jnp.float32)
    conv_all = jnp.zeros(features.shape, jnp.float32)
    for offset in range(taps_count):
        begin_at = taps_count - 1 - offset
        conv_all = (
            conv_all
            + short_taps[offset][:, :, None] * extended[:, :, begin_at : begin_at + tok_local]
        )
    query_conv = conv_all[0]
    product = (conv_all[1] * conv_all[2]).astype(jnp.bfloat16)
    gathered = lax.all_to_all(product, "ctx", split_axis=0, concat_axis=1, tiled=True)
    signal = gathered.astype(jnp.float32)
    sig_real, sig_imag = forward_dft(signal.reshape(chan_dev, half_rows, col_count), tables)
    four_shape = (group_dev, per_group, row_count, col_count)
    sig_real = sig_real.reshape(four_shape)
    sig_imag = sig_imag.reshape(four_shape)
    kernel_wide_real = kernel_real[:, None]
    kernel_wide_imag = kernel_imag[:, None]
    prod_real = (sig_real * kernel_wide_real - sig_imag * kernel_wide_imag).reshape(
        chan_dev, row_count, col_count
    )
    prod_imag = (sig_real * kernel_wide_imag + sig_imag * kernel_wide_real).reshape(
        chan_dev, row_count, col_count
    )
    longconv = inverse_dft(prod_real, prod_imag, tables, half_rows).reshape(chan_dev, seq_len)
    skip_local = lax.dynamic_slice_in_dim(skip_gain, ctx_rank * chan_dev, chan_dev, 0)
    long_mix = (longconv + skip_local[:, None] * signal).astype(jnp.bfloat16)
    restored = lax.all_to_all(long_mix, "ctx", split_axis=1, concat_axis=0, tiled=True)
    gated = (query_conv * restored.astype(jnp.float32)).astype(jnp.bfloat16)
    return lax.psum_scatter(
        lax.dot_general(
            out_weight, gated, (((0,), (0,)), ((), ())), preferred_element_type=jnp.float32
        ).astype(jnp.bfloat16),
        "tp",
        scatter_dimension=0,
        tiled=True,
    )


LANES = 128
NT = (((1,), (1,)), ((), ()))
NN = (((1,), (0,)), ((), ()))


def block_kernel(
    ctx_count, pieces, halves,
    features_hbm, short_taps_hbm, filters_hbm, skip_gain_hbm, weight_hbm, out,
    features, short_taps, filters, skip_gain, weight, weight_turned, taps_rows, taps, filters_wide, toeplitz,
    halo_tx, halo_rx, edge_rx, edge_columns, kv, kv_rx, mix_tx, mix_rx, query, gated,
    sib_tx, sib_rx, far_tx, far_rx,
    load_sem, halo_send, halo_recv, edge_send, edge_recv, kv_send, kv_recv, mix_send, mix_recv,
    sib_send, sib_recv, far_send, far_recv,
):
    loads = [
        pltpu.make_async_copy(source, target, load_sem.at[index])
        for index, (source, target) in enumerate((
            (features_hbm, features), (short_taps_hbm, short_taps), (skip_gain_hbm, skip_gain),
            (filters_hbm, filters), (weight_hbm, weight),
        ))
    ]
    for load in loads:
        load.start()
    taps_count = short_taps.shape[0]
    chan_tp, tok = features.shape[1:]
    chan_dev = chan_tp // ctx_count
    group_dev = chan_dev // GROUP
    out_dev = out.shape[0]
    me = lax.axis_index("ctx")
    rank = lax.axis_index("tp")
    core = lax.rem(rank, 2)
    sibling = rank + 1 - 2 * core
    far = lax.rem(rank + 2, 4)

    barrier = pltpu.get_barrier_semaphore()
    for step in range(1, ctx_count):
        pl.semaphore_signal(
            barrier, inc=1, device_id={"ctx": lax.rem(me + step, ctx_count)},
            device_id_type=pl.DeviceIdType.MESH,
        )
    for other in (sibling, far):
        pl.semaphore_signal(
            barrier, inc=1, device_id={"tp": other}, device_id_type=pl.DeviceIdType.MESH
        )

    taps_rows[...] = jnp.zeros_like(taps_rows)
    loads[1].wait()
    loads[2].wait()
    for offset in range(taps_count):
        taps_rows[3 * offset : 3 * offset + 3, :] = short_taps[offset]
    taps_rows[3 * taps_count : 3 * taps_count + 1, :] = skip_gain[...]
    taps[...] = taps_rows[...].T

    edges = taps_count - 1
    slots = halo_tx.shape[0]
    slot_of = lax.broadcasted_iota(jnp.int32, (slots, tok), 0)
    col_of = lax.broadcasted_iota(jnp.int32, (slots, tok), 1)
    loads[0].wait()
    edge = jnp.zeros((slots, chan_tp), jnp.float32)
    for row, first_slot, count in ((1, 0, 2 * edges), (2, 2 * edges, 2 * edges), (0, 4 * edges, edges)):
        inner = slot_of - first_slot
        wanted = jnp.where(inner < edges, tok - edges + inner, inner - edges)
        pick = (inner >= 0) & (inner < count) & (col_of == wanted)
        edge += lax.dot_general(
            pick.astype(jnp.bfloat16), features[row], NT, preferred_element_type=jnp.float32
        )
    halo_tx[...] = edge.astype(jnp.bfloat16)

    lane = lax.broadcasted_iota(jnp.int32, (chan_tp, tok), 1)

    def short_conv(row, halo):
        values = features[row].astype(jnp.float32)
        total = taps[:, row : row + 1] * values
        for offset in range(1, taps_count):
            moved = pltpu.roll(values, offset, 1)
            if halo is not None:
                for place in range(offset):
                    column = 4 * edges + edges - offset + place
                    moved = jnp.where(lane == place, halo[:, column : column + 1], moved)
            index = 3 * offset + row
            total = total + taps[:, index : index + 1] * moved
        return total

    kv[...] = (short_conv(1, None) * short_conv(2, None)).astype(jnp.bfloat16)

    pl.semaphore_wait(barrier, ctx_count + 1)

    def halo_copy():
        return pltpu.make_async_remote_copy(
            src_ref=halo_tx, dst_ref=halo_rx, send_sem=halo_send, recv_sem=halo_recv,
            device_id={"ctx": lax.rem(me + 1, ctx_count)},
            device_id_type=pl.DeviceIdType.MESH,
        )

    def tile_of(target):
        return pl.ds(pl.multiple_of(target * chan_dev // LANES * LANES, LANES), LANES)

    def edge_copy(step):
        target = lax.rem(me + step, ctx_count)
        return pltpu.make_async_remote_copy(
            src_ref=halo_tx.at[:, tile_of(target)], dst_ref=edge_rx.at[me],
            send_sem=edge_send.at[step], recv_sem=edge_recv.at[step],
            device_id={"ctx": target}, device_id_type=pl.DeviceIdType.MESH,
        )

    part = chan_dev // pieces

    def kv_copy(step, piece):
        target = lax.rem(me + step, ctx_count)
        begin = pl.multiple_of(target * chan_dev + piece * part, part)
        return pltpu.make_async_remote_copy(
            src_ref=kv.at[pl.ds(begin, part)],
            dst_ref=kv_rx.at[me, pl.ds(piece * part, part)],
            send_sem=kv_send.at[piece, step], recv_sem=kv_recv.at[piece, step],
            device_id={"ctx": target}, device_id_type=pl.DeviceIdType.MESH,
        )

    def mix_copy(step, piece):
        target = lax.rem(me + step, ctx_count)
        begin = pl.multiple_of(me * chan_dev + piece * part, part)
        return pltpu.make_async_remote_copy(
            src_ref=mix_tx.at[target, pl.ds(piece * part, part)],
            dst_ref=mix_rx.at[pl.ds(begin, part)],
            send_sem=mix_send.at[piece, step], recv_sem=mix_recv.at[piece, step],
            device_id={"ctx": target}, device_id_type=pl.DeviceIdType.MESH,
        )

    order = sorted(range(1, ctx_count), key=lambda step: -min(step, ctx_count - step))
    for piece in range(pieces):
        for step in order:
            kv_copy(step, piece).start()
        if piece == 0:
            for step in order:
                edge_copy(step).start()

    @pl.when(me < ctx_count - 1)
    def _():
        halo_copy().start()

    own = pl.ds(pl.multiple_of(me * chan_dev, chan_dev), chan_dev)
    kv_rx[me] = kv[own, :]
    edge_rx[me] = halo_tx[:, tile_of(me)]

    loads[3].wait()
    filters_wide[...] = filters[...].astype(jnp.float32)
    length = filters.shape[1]
    wide_row = lax.broadcasted_iota(jnp.int32, (tok, length), 0)
    wide_col = lax.broadcasted_iota(jnp.int32, (tok, length), 1)
    for group in range(group_dev):
        taps_long = filters_wide[pl.ds(me * group_dev + group, 1), :]
        spread = pltpu.roll(
            jnp.broadcast_to(taps_long, (tok, length)), 0, 1, stride=1, stride_axis=0
        )
        toeplitz[group] = jnp.where(wide_col >= wide_row, spread, 0.0).astype(jnp.bfloat16)

    @pl.when(me > 0)
    def _():
        halo_copy().wait_recv()

    @pl.when(me == 0)
    def _():
        halo_rx[...] = jnp.zeros_like(halo_rx)

    query[...] = short_conv(0, halo_rx[...].astype(jnp.float32).T)

    for step in order:
        edge_copy(step).wait_recv()
    spots = ctx_count * slots
    edge_columns[...] = edge_rx[...].astype(jnp.float32).reshape(spots, LANES).T
    begin = pl.multiple_of(me * chan_dev % LANES, GROUP)
    here = edge_columns[pl.ds(begin, chan_dev), :]
    spot = lax.broadcasted_iota(jnp.int32, (chan_dev, spots), 1)
    slot = spot % slots
    before = jnp.where(spot < slots, 0.0, pltpu.roll(here, slots, 1))
    series = jnp.where(slot % (2 * edges) < edges, before, here)
    own_taps = taps[own, :]
    edge_conv = jnp.zeros((chan_dev, spots), jnp.float32)
    for offset in range(taps_count):
        index = 3 * offset
        factor = jnp.where(
            slot < 2 * edges, own_taps[:, index + 1 : index + 2], own_taps[:, index + 2 : index + 3]
        )
        moved = series if offset == 0 else pltpu.roll(series, offset, 1)
        edge_conv = edge_conv + factor * moved
    mended = edge_conv * pltpu.roll(edge_conv, spots - 2 * edges, 1)
    place_of = lax.broadcasted_iota(jnp.int32, (GROUP, tok), 1)
    groups_part = group_dev // pieces
    for piece in range(pieces):
        for step in order:
            kv_copy(step, piece).wait_recv()
        for group in range(piece * groups_part, (piece + 1) * groups_part):
            rows = slice(group * GROUP, (group + 1) * GROUP)
            blocks = []
            for block in range(ctx_count):
                values = kv_rx[block, rows, :].astype(jnp.float32)
                for place in range(edges):
                    column = block * slots + edges + place
                    values = jnp.where(
                        place_of == place, mended[rows, column : column + 1], values
                    )
                blocks.append(values.astype(jnp.bfloat16))
            signal = jnp.concatenate(blocks, axis=0)
            begin = pl.multiple_of(me * chan_dev + group * GROUP, GROUP)
            column = 3 * taps_count
            direct = taps[pl.ds(begin, GROUP), :][:, column : column + 1]
            totals = [
                direct * blocks[block].astype(jnp.float32) for block in range(ctx_count)
            ]
            wide = 2 if ctx_count % 2 == 0 else 1
            for distance in range(0, ctx_count, wide):
                products = lax.dot_general(
                    signal[: (ctx_count - distance) * GROUP],
                    toeplitz[group, :, distance * tok : (distance + wide) * tok],
                    NN, preferred_element_type=jnp.float32,
                )
                for more in range(wide):
                    for block in range(distance + more, ctx_count):
                        source = block - distance - more
                        totals[block] += products[
                            source * GROUP : (source + 1) * GROUP, more * tok : (more + 1) * tok
                        ]
            for block in range(ctx_count):
                mix_tx[block, rows, :] = totals[block].astype(jnp.bfloat16)
        for step in order:
            mix_copy(step, piece).start()
    mix_rx[own, :] = mix_tx[me]
    loads[4].wait()
    turn = 256

    @pl.loop(0, weight.shape[1] // turn)
    def _(index):
        begin = pl.multiple_of(index * turn, turn)
        weight_turned[pl.ds(begin, turn), :] = weight[:, pl.ds(begin, turn)].T

    for piece in range(pieces):
        for step in order:
            mix_copy(step, piece).wait_recv()
    gated[...] = (query[...] * mix_rx[...].astype(jnp.float32)).astype(jnp.bfloat16)

    rows_half = out_dev // halves

    def partial(owner, half):
        begin = pl.multiple_of(owner * out_dev + half * rows_half, rows_half)
        return lax.dot_general(
            weight_turned[pl.ds(begin, rows_half), :], gated[...], NN,
            preferred_element_type=jnp.float32,
        )

    def half_of(half):
        return pl.ds(half * rows_half, rows_half)

    def sib_copy(slot, half):
        return pltpu.make_async_remote_copy(
            src_ref=sib_tx.at[slot, half_of(half)], dst_ref=sib_rx.at[slot, half_of(half)],
            send_sem=sib_send.at[slot, half], recv_sem=sib_recv.at[slot, half],
            device_id={"tp": sibling}, device_id_type=pl.DeviceIdType.MESH,
        )

    def far_copy(half):
        return pltpu.make_async_remote_copy(
            src_ref=far_tx.at[half_of(half)], dst_ref=far_rx.at[half_of(half)],
            send_sem=far_send.at[half], recv_sem=far_recv.at[half],
            device_id={"tp": far}, device_id_type=pl.DeviceIdType.MESH,
        )

    far_sibling = lax.rem(sibling + 2, 4)
    for half in range(halves):
        sib_tx[0, half_of(half), :] = partial(far_sibling, half).astype(jnp.bfloat16)
        sib_copy(0, half).start()
    for half in range(halves):
        mine = partial(far, half)
        sib_copy(0, half).wait_recv()
        far_tx[half_of(half), :] = (
            mine + sib_rx[0, half_of(half), :].astype(jnp.float32)
        ).astype(jnp.bfloat16)
        far_copy(half).start()
    for half in range(halves):
        sib_tx[1, half_of(half), :] = partial(sibling, half).astype(jnp.bfloat16)
        sib_copy(1, half).start()
    for half in range(halves):
        mine = partial(rank, half)
        sib_copy(1, half).wait_recv()
        mine += sib_rx[1, half_of(half), :].astype(jnp.float32)
        far_copy(half).wait_recv()
        out[half_of(half), :] = (
            mine + far_rx[half_of(half), :].astype(jnp.float32)
        ).astype(jnp.bfloat16)

    @pl.when(me < ctx_count - 1)
    def _():
        halo_copy().wait_send()

    for step in order:
        edge_copy(step).wait_send()
    for piece in range(pieces):
        for step in order:
            kv_copy(step, piece).wait_send()
            mix_copy(step, piece).wait_send()
    for half in range(halves):
        sib_copy(0, half).wait_send()
        sib_copy(1, half).wait_send()
        far_copy(half).wait_send()


def fused(features, short_taps, filters, skip_gain, out_weight):
    taps_count = short_taps.shape[0]
    _, chan_tp, tok = features.shape
    ctx_count = lax.axis_size("ctx")
    group_rows, length = filters.shape
    chan_dev = chan_tp // ctx_count
    group_dev = chan_dev // GROUP
    out_all = out_weight.shape[1]
    out_dev = out_all // lax.axis_size("tp")
    pieces = 2 if group_dev % 2 == 0 else 1
    halves = 2
    bf16, f32 = jnp.bfloat16, jnp.float32
    dma = pltpu.SemaphoreType.DMA
    return pl.pallas_call(
        functools.partial(block_kernel, ctx_count, pieces, halves),
        out_shape=jax.ShapeDtypeStruct((out_dev, tok), bf16),
        in_specs=[pl.BlockSpec(memory_space=pltpu.HBM)] * 5,
        out_specs=pl.BlockSpec(memory_space=pltpu.VMEM),
        scratch_shapes=[
            pltpu.VMEM(features.shape, bf16),
            pltpu.VMEM(short_taps.shape, f32),
            pltpu.VMEM(filters.shape, bf16),
            pltpu.VMEM((1, chan_tp), f32),
            pltpu.VMEM((chan_tp, out_all), bf16),
            pltpu.VMEM((out_all, chan_tp), bf16),
            pltpu.VMEM((16, chan_tp), f32),
            pltpu.VMEM((chan_tp, 16), f32),
            pltpu.VMEM((group_rows, length), f32),
            pltpu.VMEM((group_dev, tok, length), bf16),
            pltpu.VMEM((16, chan_tp), bf16),
            pltpu.VMEM((16, chan_tp), bf16),
            pltpu.VMEM((ctx_count, 16, LANES), bf16),
            pltpu.VMEM((LANES, ctx_count * 16), f32),
            pltpu.VMEM((chan_tp, tok), bf16),
            pltpu.VMEM((ctx_count, chan_dev, tok), bf16),
            pltpu.VMEM((ctx_count, chan_dev, tok), bf16),
            pltpu.VMEM((chan_tp, tok), bf16),
            pltpu.VMEM((chan_tp, tok), f32),
            pltpu.VMEM((chan_tp, tok), bf16),
            pltpu.VMEM((2, out_dev, tok), bf16),
            pltpu.VMEM((2, out_dev, tok), bf16),
            pltpu.VMEM((out_dev, tok), bf16),
            pltpu.VMEM((out_dev, tok), bf16),
            dma((5,)), dma, dma,
            dma((ctx_count,)), dma((ctx_count,)),
            dma((pieces, ctx_count)), dma((pieces, ctx_count)),
            dma((pieces, ctx_count)), dma((pieces, ctx_count)),
            dma((2, halves)), dma((2, halves)),
            dma((halves,)), dma((halves,)),
        ],
        compiler_params=pltpu.CompilerParams(
            collective_id=0, has_side_effects=True, vmem_limit_bytes=40 * 2**20
        ),
    )(*(
        pltpu.with_memory_space_constraint(value, pltpu.HBM)
        for value in (features, short_taps, filters, skip_gain.reshape(1, chan_tp), out_weight)
    ))


def fits_kernel(mesh, features, short_taps, filters, skip_gain, out_weight):
    ctx_count, tp_count = mesh.shape["ctx"], mesh.shape["tp"]
    rows, channels, tokens = features.shape
    taps_count = short_taps.shape[0]
    tok = tokens // ctx_count
    chan_tp = channels // tp_count
    toeplitz_bytes = chan_tp // ctx_count // GROUP * tok * tokens * 2
    return (
        tp_count == 4
        and tok == LANES
        and 5 * (taps_count - 1) <= 16
        and ctx_count * 16 % LANES == 0
        and LANES % (chan_tp // ctx_count) == 0
        and rows * taps_count < 16
        and chan_tp % (ctx_count * GROUP) == 0
        and chan_tp % LANES == 0
        and out_weight.shape[1] % (tp_count * 256) == 0
        and toeplitz_bytes <= 2**22
    )


def solution(mesh):
    placed = (P(None, "tp", "ctx"), P(None, None, "tp"), P("tp", None), P("tp"), P("tp", None))

    def run(*arrays):
        body = fused if fits_kernel(mesh, *arrays) else local
        return jax.shard_map(
            body, mesh=mesh, in_specs=placed, out_specs=P("tp", "ctx"), check_vma=False
        )(*arrays)

    return run
```

```python
import functools
import math

import jax
import jax.numpy as jnp
from jax import lax
from jax.experimental import pallas as pl
from jax.experimental.pallas import tpu as pltpu
from jax.sharding import PartitionSpec as P

GROUP = 16


highest = lax.Precision.HIGHEST


def from_behind(value, axis, steps):
    count = lax.axis_size(axis)
    initial, last = (max(0, -steps), min(count, count - steps))
    return lax.ppermute(value, axis, [(source, source + steps) for source in range(initial, last)])


def left_product(matrix, stacked):
    return jnp.einsum("kn,bns->bks", matrix, stacked, precision=highest)


def right_product(stacked, matrix):
    return jnp.einsum("bks,st->bkt", stacked, matrix, precision=highest)


def split_length(total_len):
    row_count = 2
    for candidate in range(2, math.isqrt(total_len) + 1, 2):
        if total_len % candidate == 0:
            row_count = candidate
    return (row_count, total_len // row_count)


def dft_tables(row_count, col_count):
    total_len = row_count * col_count
    row_index = jnp.arange(row_count, dtype=jnp.int32)
    col_index = jnp.arange(col_count, dtype=jnp.int32)
    row_angle = (row_index[:, None] * row_index[None, :] % row_count).astype(jnp.float32) * (
        2.0 * math.pi / row_count
    )
    col_angle = (col_index[:, None] * col_index[None, :] % col_count).astype(jnp.float32) * (
        2.0 * math.pi / col_count
    )
    twist_angle = (row_index[:, None] * col_index[None, :] % total_len).astype(jnp.float32) * (
        2.0 * math.pi / total_len
    )
    return (
        jnp.cos(row_angle),
        jnp.sin(row_angle),
        jnp.cos(col_angle),
        jnp.sin(col_angle),
        jnp.cos(twist_angle),
        jnp.sin(twist_angle),
    )


def forward_dft(signal, tables):
    cos_row, sin_row, cos_col, sin_col, cos_twist, sin_twist = tables
    half_rows = signal.shape[1]
    first_real = left_product(cos_row[:, :half_rows], signal)
    first_imag = -left_product(sin_row[:, :half_rows], signal)
    twist_real = first_real * cos_twist + first_imag * sin_twist
    twist_imag = first_imag * cos_twist - first_real * sin_twist
    spec_real = right_product(twist_real, cos_col) + right_product(twist_imag, sin_col)
    spec_imag = right_product(twist_imag, cos_col) - right_product(twist_real, sin_col)
    return (spec_real, spec_imag)


def inverse_dft(spec_real, spec_imag, tables, half_rows):
    cos_row, sin_row, cos_col, sin_col, cos_twist, sin_twist = tables
    total_len = cos_row.shape[0] * cos_col.shape[0]
    middle_real = right_product(spec_real, cos_col) - right_product(spec_imag, sin_col)
    middle_imag = right_product(spec_imag, cos_col) + right_product(spec_real, sin_col)
    turned_real = middle_real * cos_twist - middle_imag * sin_twist
    turned_imag = middle_imag * cos_twist + middle_real * sin_twist
    signal = left_product(cos_row[:half_rows, :], turned_real) - left_product(
        sin_row[:half_rows, :], turned_imag
    )
    return signal / total_len


def local(features, short_taps, filters, skip_gain, out_weight):
    taps_count = short_taps.shape[0]
    chan_tp = features.shape[1]
    tok_local = features.shape[2]
    ctx_count = lax.axis_size("ctx")
    chan_dev = chan_tp // ctx_count
    group_dev = max(1, chan_dev // GROUP)
    per_group = chan_dev // group_dev
    seq_len = tok_local * ctx_count
    row_count, col_count = split_length(2 * seq_len)
    half_rows = row_count // 2
    tables = dft_tables(row_count, col_count)
    ctx_rank = lax.axis_index("ctx")
    kernel_rows = lax.dynamic_slice_in_dim(filters, ctx_rank * chan_dev // GROUP, group_dev, 0)
    kernel_real, kernel_imag = forward_dft(
        kernel_rows.astype(jnp.float32).reshape(group_dev, half_rows, col_count), tables
    )
    previous = from_behind(features[:, :, tok_local - (taps_count - 1) :], "ctx", 1)
    extended = jnp.concatenate([previous, features], axis=2).astype(jnp.float32)
    conv_all = jnp.zeros(features.shape, jnp.float32)
    for offset in range(taps_count):
        begin_at = taps_count - 1 - offset
        conv_all = (
            conv_all
            + short_taps[offset][:, :, None] * extended[:, :, begin_at : begin_at + tok_local]
        )
    query_conv = conv_all[0]
    product = (conv_all[1] * conv_all[2]).astype(jnp.bfloat16)
    gathered = lax.all_to_all(product, "ctx", split_axis=0, concat_axis=1, tiled=True)
    signal = gathered.astype(jnp.float32)
    sig_real, sig_imag = forward_dft(signal.reshape(chan_dev, half_rows, col_count), tables)
    four_shape = (group_dev, per_group, row_count, col_count)
    sig_real = sig_real.reshape(four_shape)
    sig_imag = sig_imag.reshape(four_shape)
    kernel_wide_real = kernel_real[:, None]
    kernel_wide_imag = kernel_imag[:, None]
    prod_real = (sig_real * kernel_wide_real - sig_imag * kernel_wide_imag).reshape(
        chan_dev, row_count, col_count
    )
    prod_imag = (sig_real * kernel_wide_imag + sig_imag * kernel_wide_real).reshape(
        chan_dev, row_count, col_count
    )
    longconv = inverse_dft(prod_real, prod_imag, tables, half_rows).reshape(chan_dev, seq_len)
    skip_local = lax.dynamic_slice_in_dim(skip_gain, ctx_rank * chan_dev, chan_dev, 0)
    long_mix = (longconv + skip_local[:, None] * signal).astype(jnp.bfloat16)
    restored = lax.all_to_all(long_mix, "ctx", split_axis=1, concat_axis=0, tiled=True)
    gated = (query_conv * restored.astype(jnp.float32)).astype(jnp.bfloat16)
    return lax.psum_scatter(
        lax.dot_general(
            out_weight, gated, (((0,), (0,)), ((), ())), preferred_element_type=jnp.float32
        ).astype(jnp.bfloat16),
        "tp",
        scatter_dimension=0,
        tiled=True,
    )


LANES = 128
NT = (((1,), (1,)), ((), ()))
NN = (((1,), (0,)), ((), ()))


def block_kernel(
    ctx_count, pieces, halves,
    features_hbm, short_taps_hbm, filters_hbm, skip_gain_hbm, weight_hbm, out,
    features, short_taps, filters, skip_gain, weight, weight_turned, taps_rows, taps, filters_wide, toeplitz,
    halo_tx, halo_rx, edge_rx, edge_columns, kv, kv_rx, mix_tx, mix_rx, query, gated,
    sib_tx, sib_rx, far_tx, far_rx,
    load_sem, halo_send, halo_recv, edge_send, edge_recv, kv_send, kv_recv, mix_send, mix_recv,
    sib_send, sib_recv, far_send, far_recv,
):
    loads = [
        pltpu.make_async_copy(source, target, load_sem.at[index])
        for index, (source, target) in enumerate((
            (features_hbm, features), (short_taps_hbm, short_taps), (skip_gain_hbm, skip_gain),
            (filters_hbm, filters), (weight_hbm, weight),
        ))
    ]
    loads[0].start()
    taps_count = short_taps.shape[0]
    chan_tp, tok = features.shape[1:]
    chan_dev = chan_tp // ctx_count
    group_dev = chan_dev // GROUP
    out_dev = out.shape[0]
    me = lax.axis_index("ctx")
    rank = lax.axis_index("tp")
    core = lax.rem(rank, 2)
    sibling = rank + 1 - 2 * core
    far = lax.rem(rank + 2, 4)

    barrier = pltpu.get_barrier_semaphore()
    for step in range(1, ctx_count):
        pl.semaphore_signal(
            barrier, inc=1, device_id={"ctx": lax.rem(me + step, ctx_count)},
            device_id_type=pl.DeviceIdType.MESH,
        )
    for other in (sibling, far):
        pl.semaphore_signal(
            barrier, inc=1, device_id={"tp": other}, device_id_type=pl.DeviceIdType.MESH
        )

    for load in loads[1:]:
        load.start()

    taps_rows[...] = jnp.zeros_like(taps_rows)
    loads[1].wait()
    loads[2].wait()
    for offset in range(taps_count):
        taps_rows[3 * offset : 3 * offset + 3, :] = short_taps[offset]
    taps_rows[3 * taps_count : 3 * taps_count + 1, :] = skip_gain[...]
    taps[...] = taps_rows[...].T

    edges = taps_count - 1
    slots = halo_tx.shape[0]
    lane = lax.broadcasted_iota(jnp.int32, (chan_tp, tok), 1)

    def short_conv(row, halo):
        values = features[row].astype(jnp.float32)
        total = taps[:, row : row + 1] * values
        for offset in range(1, taps_count):
            moved = pltpu.roll(values, offset, 1)
            if halo is not None:
                for place in range(offset):
                    column = 4 * edges + edges - offset + place
                    moved = jnp.where(lane == place, halo[:, column : column + 1], moved)
            index = 3 * offset + row
            total = total + taps[:, index : index + 1] * moved
        return total

    loads[0].wait()

    kv[...] = (short_conv(1, None) * short_conv(2, None)).astype(jnp.bfloat16)

    pl.semaphore_wait(barrier, ctx_count + 1)

    def halo_copy():
        return pltpu.make_async_remote_copy(
            src_ref=halo_tx, dst_ref=halo_rx, send_sem=halo_send, recv_sem=halo_recv,
            device_id={"ctx": lax.rem(me + 1, ctx_count)},
            device_id_type=pl.DeviceIdType.MESH,
        )

    def tile_of(target):
        return pl.ds(pl.multiple_of(target * chan_dev // LANES * LANES, LANES), LANES)

    def edge_copy(step):
        target = lax.rem(me + step, ctx_count)
        return pltpu.make_async_remote_copy(
            src_ref=halo_tx.at[:, tile_of(target)], dst_ref=edge_rx.at[me],
            send_sem=edge_send.at[step], recv_sem=edge_recv.at[step],
            device_id={"ctx": target}, device_id_type=pl.DeviceIdType.MESH,
        )

    part = chan_dev // pieces

    def kv_copy(step, piece):
        target = lax.rem(me + step, ctx_count)
        begin = pl.multiple_of(target * chan_dev + piece * part, part)
        return pltpu.make_async_remote_copy(
            src_ref=kv.at[pl.ds(begin, part)],
            dst_ref=kv_rx.at[me, pl.ds(piece * part, part)],
            send_sem=kv_send.at[piece, step], recv_sem=kv_recv.at[piece, step],
            device_id={"ctx": target}, device_id_type=pl.DeviceIdType.MESH,
        )

    def mix_copy(step, piece):
        target = lax.rem(me + step, ctx_count)
        begin = pl.multiple_of(me * chan_dev + piece * part, part)
        return pltpu.make_async_remote_copy(
            src_ref=mix_tx.at[target, pl.ds(piece * part, part)],
            dst_ref=mix_rx.at[pl.ds(begin, part)],
            send_sem=mix_send.at[piece, step], recv_sem=mix_recv.at[piece, step],
            device_id={"ctx": target}, device_id_type=pl.DeviceIdType.MESH,
        )

    order = sorted(range(1, ctx_count), key=lambda step: -min(step, ctx_count - step))
    for piece in range(pieces):
        for step in order:
            kv_copy(step, piece).start()
        if piece == 0:
            slot_of = lax.broadcasted_iota(jnp.int32, (slots, tok), 0)
            col_of = lax.broadcasted_iota(jnp.int32, (slots, tok), 1)
            edge = jnp.zeros((slots, chan_tp), jnp.float32)
            for row, first_slot, count in ((1, 0, 2 * edges), (2, 2 * edges, 2 * edges), (0, 4 * edges, edges)):
                inner = slot_of - first_slot
                wanted = jnp.where(inner < edges, tok - edges + inner, inner - edges)
                pick = (inner >= 0) & (inner < count) & (col_of == wanted)
                edge += lax.dot_general(
                    pick.astype(jnp.bfloat16), features[row], NT, preferred_element_type=jnp.float32
                )
            halo_tx[...] = edge.astype(jnp.bfloat16)
            for step in order:
                edge_copy(step).start()

    @pl.when(me < ctx_count - 1)
    def _():
        halo_copy().start()

    own = pl.ds(pl.multiple_of(me * chan_dev, chan_dev), chan_dev)
    kv_rx[me] = kv[own, :]
    edge_rx[me] = halo_tx[:, tile_of(me)]

    loads[3].wait()
    filters_wide[...] = filters[...].astype(jnp.float32)
    length = filters.shape[1]
    wide_row = lax.broadcasted_iota(jnp.int32, (tok, length), 0)
    wide_col = lax.broadcasted_iota(jnp.int32, (tok, length), 1)
    for group in range(group_dev):
        taps_long = filters_wide[pl.ds(me * group_dev + group, 1), :]
        spread = pltpu.roll(
            jnp.broadcast_to(taps_long, (tok, length)), 0, 1, stride=1, stride_axis=0
        )
        toeplitz[group] = jnp.where(wide_col >= wide_row, spread, 0.0).astype(jnp.bfloat16)

    @pl.when(me > 0)
    def _():
        halo_copy().wait_recv()

    @pl.when(me == 0)
    def _():
        halo_rx[...] = jnp.zeros_like(halo_rx)

    query[...] = short_conv(0, halo_rx[...].astype(jnp.float32).T)

    for step in order:
        edge_copy(step).wait_recv()
    spots = ctx_count * slots
    edge_columns[...] = edge_rx[...].astype(jnp.float32).reshape(spots, LANES).T
    begin = pl.multiple_of(me * chan_dev % LANES, GROUP)
    here = edge_columns[pl.ds(begin, chan_dev), :]
    spot = lax.broadcasted_iota(jnp.int32, (chan_dev, spots), 1)
    slot = spot % slots
    before = jnp.where(spot < slots, 0.0, pltpu.roll(here, slots, 1))
    series = jnp.where(slot % (2 * edges) < edges, before, here)
    own_taps = taps[own, :]
    edge_conv = jnp.zeros((chan_dev, spots), jnp.float32)
    for offset in range(taps_count):
        index = 3 * offset
        factor = jnp.where(
            slot < 2 * edges, own_taps[:, index + 1 : index + 2], own_taps[:, index + 2 : index + 3]
        )
        moved = series if offset == 0 else pltpu.roll(series, offset, 1)
        edge_conv = edge_conv + factor * moved
    mended = edge_conv * pltpu.roll(edge_conv, spots - 2 * edges, 1)
    place_of = lax.broadcasted_iota(jnp.int32, (GROUP, tok), 1)
    groups_part = group_dev // pieces
    for piece in range(pieces):
        for step in order:
            kv_copy(step, piece).wait_recv()
        for group in range(piece * groups_part, (piece + 1) * groups_part):
            rows = slice(group * GROUP, (group + 1) * GROUP)
            blocks = []
            for block in range(ctx_count):
                values = kv_rx[block, rows, :].astype(jnp.float32)
                for place in range(edges):
                    column = block * slots + edges + place
                    values = jnp.where(
                        place_of == place, mended[rows, column : column + 1], values
                    )
                blocks.append(values.astype(jnp.bfloat16))
            signal = jnp.concatenate(blocks, axis=0)
            begin = pl.multiple_of(me * chan_dev + group * GROUP, GROUP)
            column = 3 * taps_count
            direct = taps[pl.ds(begin, GROUP), :][:, column : column + 1]
            totals = [
                direct * blocks[block].astype(jnp.float32) for block in range(ctx_count)
            ]
            wide = 2 if ctx_count % 2 == 0 else 1
            for distance in range(0, ctx_count, wide):
                products = lax.dot_general(
                    signal[: (ctx_count - distance) * GROUP],
                    toeplitz[group, :, distance * tok : (distance + wide) * tok],
                    NN, preferred_element_type=jnp.float32,
                )
                for more in range(wide):
                    for block in range(distance + more, ctx_count):
                        source = block - distance - more
                        totals[block] += products[
                            source * GROUP : (source + 1) * GROUP, more * tok : (more + 1) * tok
                        ]
            for block in range(ctx_count):
                mix_tx[block, rows, :] = totals[block].astype(jnp.bfloat16)
        for step in order:
            mix_copy(step, piece).start()
    mix_rx[own, :] = mix_tx[me]
    loads[4].wait()
    turn = 256

    @pl.loop(0, weight.shape[1] // turn)
    def _(index):
        begin = pl.multiple_of(index * turn, turn)
        weight_turned[pl.ds(begin, turn), :] = weight[:, pl.ds(begin, turn)].T

    for piece in range(pieces):
        for step in order:
            mix_copy(step, piece).wait_recv()
    gated[...] = (query[...] * mix_rx[...].astype(jnp.float32)).astype(jnp.bfloat16)

    rows_half = out_dev // halves

    def partial(owner, half):
        begin = pl.multiple_of(owner * out_dev + half * rows_half, rows_half)
        return lax.dot_general(
            weight_turned[pl.ds(begin, rows_half), :], gated[...], NN,
            preferred_element_type=jnp.float32,
        )

    def half_of(half):
        return pl.ds(half * rows_half, rows_half)

    def sib_copy(slot, half):
        return pltpu.make_async_remote_copy(
            src_ref=sib_tx.at[slot, half_of(half)], dst_ref=sib_rx.at[slot, half_of(half)],
            send_sem=sib_send.at[slot, half], recv_sem=sib_recv.at[slot, half],
            device_id={"tp": sibling}, device_id_type=pl.DeviceIdType.MESH,
        )

    def far_copy(half):
        return pltpu.make_async_remote_copy(
            src_ref=far_tx.at[half_of(half)], dst_ref=far_rx.at[half_of(half)],
            send_sem=far_send.at[half], recv_sem=far_recv.at[half],
            device_id={"tp": far}, device_id_type=pl.DeviceIdType.MESH,
        )

    far_sibling = lax.rem(sibling + 2, 4)
    for half in range(halves):
        sib_tx[0, half_of(half), :] = partial(far_sibling, half).astype(jnp.bfloat16)
        sib_copy(0, half).start()
    for half in range(halves):
        mine = partial(far, half)
        sib_copy(0, half).wait_recv()
        far_tx[half_of(half), :] = (
            mine + sib_rx[0, half_of(half), :].astype(jnp.float32)
        ).astype(jnp.bfloat16)
        far_copy(half).start()
    for half in range(halves):
        sib_tx[1, half_of(half), :] = partial(sibling, half).astype(jnp.bfloat16)
        sib_copy(1, half).start()
    for half in range(halves):
        mine = partial(rank, half)
        sib_copy(1, half).wait_recv()
        mine += sib_rx[1, half_of(half), :].astype(jnp.float32)
        far_copy(half).wait_recv()
        out[half_of(half), :] = (
            mine + far_rx[half_of(half), :].astype(jnp.float32)
        ).astype(jnp.bfloat16)

    @pl.when(me < ctx_count - 1)
    def _():
        halo_copy().wait_send()

    for step in order:
        edge_copy(step).wait_send()
    for piece in range(pieces):
        for step in order:
            kv_copy(step, piece).wait_send()
            mix_copy(step, piece).wait_send()
    for half in range(halves):
        sib_copy(0, half).wait_send()
        sib_copy(1, half).wait_send()
        far_copy(half).wait_send()


def fused(features, short_taps, filters, skip_gain, out_weight):
    taps_count = short_taps.shape[0]
    _, chan_tp, tok = features.shape
    ctx_count = lax.axis_size("ctx")
    group_rows, length = filters.shape
    chan_dev = chan_tp // ctx_count
    group_dev = chan_dev // GROUP
    out_all = out_weight.shape[1]
    out_dev = out_all // lax.axis_size("tp")
    pieces = 2 if group_dev % 2 == 0 else 1
    halves = 2
    bf16, f32 = jnp.bfloat16, jnp.float32
    dma = pltpu.SemaphoreType.DMA
    return pl.pallas_call(
        functools.partial(block_kernel, ctx_count, pieces, halves),
        out_shape=jax.ShapeDtypeStruct((out_dev, tok), bf16),
        in_specs=[pl.BlockSpec(memory_space=pltpu.HBM)] * 5,
        out_specs=pl.BlockSpec(memory_space=pltpu.VMEM),
        scratch_shapes=[
            pltpu.VMEM(features.shape, bf16),
            pltpu.VMEM(short_taps.shape, f32),
            pltpu.VMEM(filters.shape, bf16),
            pltpu.VMEM((1, chan_tp), f32),
            pltpu.VMEM((chan_tp, out_all), bf16),
            pltpu.VMEM((out_all, chan_tp), bf16),
            pltpu.VMEM((16, chan_tp), f32),
            pltpu.VMEM((chan_tp, 16), f32),
            pltpu.VMEM((group_rows, length), f32),
            pltpu.VMEM((group_dev, tok, length), bf16),
            pltpu.VMEM((16, chan_tp), bf16),
            pltpu.VMEM((16, chan_tp), bf16),
            pltpu.VMEM((ctx_count, 16, LANES), bf16),
            pltpu.VMEM((LANES, ctx_count * 16), f32),
            pltpu.VMEM((chan_tp, tok), bf16),
            pltpu.VMEM((ctx_count, chan_dev, tok), bf16),
            pltpu.VMEM((ctx_count, chan_dev, tok), bf16),
            pltpu.VMEM((chan_tp, tok), bf16),
            pltpu.VMEM((chan_tp, tok), f32),
            pltpu.VMEM((chan_tp, tok), bf16),
            pltpu.VMEM((2, out_dev, tok), bf16),
            pltpu.VMEM((2, out_dev, tok), bf16),
            pltpu.VMEM((out_dev, tok), bf16),
            pltpu.VMEM((out_dev, tok), bf16),
            dma((5,)), dma, dma,
            dma((ctx_count,)), dma((ctx_count,)),
            dma((pieces, ctx_count)), dma((pieces, ctx_count)),
            dma((pieces, ctx_count)), dma((pieces, ctx_count)),
            dma((2, halves)), dma((2, halves)),
            dma((halves,)), dma((halves,)),
        ],
        compiler_params=pltpu.CompilerParams(
            collective_id=0, has_side_effects=True, vmem_limit_bytes=40 * 2**20
        ),
    )(*(
        pltpu.with_memory_space_constraint(value, pltpu.HBM)
        for value in (features, short_taps, filters, skip_gain.reshape(1, chan_tp), out_weight)
    ))


def fits_kernel(mesh, features, short_taps, filters, skip_gain, out_weight):
    ctx_count, tp_count = mesh.shape["ctx"], mesh.shape["tp"]
    rows, channels, tokens = features.shape
    taps_count = short_taps.shape[0]
    tok = tokens // ctx_count
    chan_tp = channels // tp_count
    toeplitz_bytes = chan_tp // ctx_count // GROUP * tok * tokens * 2
    return (
        tp_count == 4
        and tok == LANES
        and 5 * (taps_count - 1) <= 16
        and ctx_count * 16 % LANES == 0
        and LANES % (chan_tp // ctx_count) == 0
        and rows * taps_count < 16
        and chan_tp % (ctx_count * GROUP) == 0
        and chan_tp % LANES == 0
        and out_weight.shape[1] % (tp_count * 256) == 0
        and toeplitz_bytes <= 2**22
    )


def solution(mesh):
    placed = (P(None, "tp", "ctx"), P(None, None, "tp"), P("tp", None), P("tp"), P("tp", None))

    def run(*arrays):
        body = fused if fits_kernel(mesh, *arrays) else local
        return jax.shard_map(
            body, mesh=mesh, in_specs=placed, out_specs=P("tp", "ctx"), check_vma=False
        )(*arrays)

    return run
```
